128 devices in a mesh: tv: 16 (over z, x_hi, core), sv: 8 (over x_lo, y).
Axes of the slice: x: 4 (x_hi: 2, x_lo: 2; x = x_hi * 2 + x_lo), y: 4, z: 4, core: 2. Of those that a mesh axis runs over, the one named last changes fastest.
Arguments:
- teacher_hidden: bfloat16 [1024, 4096], P('tv', 'sv'), may hold values from -250 to 250
- student_hidden: bfloat16 [1024, 5120], P('sv', 'tv'), may hold values from -250 to 250
- teacher_head: bfloat16 [4096, 151936], P('sv', 'tv'), may hold values from -0.09375 to 0.09375
- student_head: bfloat16 [5120, 151936], P('tv', 'sv'), may hold values from -0.078125 to 0.078125
- token_ids: int32 [1024], P('tv'), may hold values from 0 to 151935
Outputs:
- rewards: float32 [1024], P('tv')
- kl_div: float32 [1024], P('tv')
- logit_grad: bfloat16 [1024, 151936], P('tv', 'sv')
The draws below stay inside these ranges and needn't reach their ends.
All inputs are finite; a program needn't handle non-finite values.
Results may differ from the reference program's by a relative error of at most 0.0042.
Values may be sent and summed in bfloat16 or wider, within the bound.
No kernel may reach another device: no remote copies, remote signals or barrier semaphores. Data moves between devices by JAX's collectives and lax.ppermute only.
A program may use at most 320 MiB of HBM per device.

```python
import math
import jax
import jax.numpy as jnp
import numpy as np

DT = 4096
DS = 5120
V = 151936
TOKENS = 1024


def scaled_rows(key, row_total, col_total, low, high, spike):
    key_values, key_scales, key_phase = jax.random.split(key, 3)
    values = jnp.clip(jax.random.normal(key_values, (row_total, col_total), jnp.float32), -4.0, 4.0)
    scales = jnp.exp(jax.random.uniform(key_scales, (row_total, 1), jnp.float32, math.log(low), math.log(high)))
    phase = jax.random.randint(key_phase, (), 0, 29)
    row_index = jnp.arange(row_total)[:, None]
    scales = jnp.where(row_index % 29 == phase, spike, scales)
    return (values * scales).astype(jnp.bfloat16)


def draw_teacher_hidden(key, part):
    key = jax.random.fold_in(key, 11)
    return scaled_rows(key, TOKENS, DT, 0.3, 3.0, 1.0)


def draw_student_hidden(key, part):
    key = jax.random.fold_in(key, 23)
    return scaled_rows(key, TOKENS, DS, 0.3, 3.0, 1.0)


def touch_ends(drawn, rng, smallest, high):
    index_at = [jax.random.randint(jax.random.fold_in(rng, axis), (), 0, length) for axis, length in enumerate(drawn.shape)]
    widest = drawn.shape.index(max(drawn.shape))
    neighbour = index_at[:widest] + [(index_at[widest] + 1) % drawn.shape[widest]] + index_at[widest + 1:]
    return drawn.at[tuple(index_at)].set(smallest).at[tuple(neighbour)].set(high)


def level_of(key, dims, shards, low, top_value):
    factor_of = 1.0
    for position, blocks in shards:
        heights = jax.random.uniform(jax.random.fold_in(jax.random.fold_in(key, 6), position), (blocks,), jnp.float32, low / len(shards), top_value / len(shards))
        factor_of = factor_of * jnp.repeat(jnp.exp(heights), dims[position] // blocks).reshape((-1,) + (1,) * (len(dims) - 1 - position))
    return factor_of


def skewed_wide(stream_key, dims, amount, lean):
    loads = [min(1 << octave, amount + 1 - (1 << octave)) * (1 << 20) // math.isqrt((1 << octave) ** lean) + 1 for octave in range((amount + 1).bit_length()) if 1 << octave <= amount]
    scale = 1 + sum(loads) // (1 << 30)
    grid = np.cumsum(np.array([max(1, weight // scale) for weight in loads]))
    lot = jax.random.randint(jax.random.fold_in(stream_key, 1), dims, 0, int(grid[len(loads) - 1]))
    start = jnp.left_shift(1, jnp.searchsorted(jnp.asarray(grid, jnp.int32), lot, side="right").astype(jnp.int32))
    rank = start - 1 + jax.random.randint(jax.random.fold_in(stream_key, 4), dims, 0, 1 << 30) % jnp.minimum(start, amount + 1 - start)
    return jax.random.permutation(jax.random.fold_in(stream_key, 2), amount)[rank].astype(jnp.int32)


def gaussian(rng, shape, deviation, most, cuts=(), kind=jnp.bfloat16):
    result = jax.random.normal(rng, shape, jnp.float32) * deviation
    if len(cuts) > 0:
        result = level_of(rng, shape, cuts, -0.22, 0.18) * result
    return jnp.clip(result, min=-most, max=most).astype(kind)


def setup_inputs(seed: int = 0) -> dict:
    seeds = jax.random.split(jax.random.key(seed), 6)
    teacher_hidden = draw_teacher_hidden(jax.random.fold_in(seeds[5], 71), 0)
    student_hidden = draw_student_hidden(jax.random.fold_in(seeds[5], 71), 0)
    teacher_head = gaussian(seeds[2], (DT, V), DT ** -0.5, 0.09375, ((0, 8), (1, 16)))
    student_head = gaussian(seeds[3], (DS, V), DS ** -0.5, 0.078125, ((0, 16), (1, 8)))
    token_ids = touch_ends(skewed_wide(seeds[4], (TOKENS,), V, 2), jax.random.fold_in(seeds[4], 3), 0, V - 1).astype(jnp.int32)
    return {"teacher_hidden": teacher_hidden, "student_hidden": student_hidden, "teacher_head": teacher_head, "student_head": student_head, "token_ids": token_ids}


def reference(teacher_hidden, student_hidden, teacher_head, student_head, token_ids):
    teacher_logits = jnp.dot(teacher_hidden, teacher_head, preferred_element_type=jnp.float32).astype(jnp.bfloat16)
    student_logits = jnp.dot(student_hidden, student_head, preferred_element_type=jnp.float32)
    teacher_wide = teacher_logits.astype(jnp.float32)
    teacher_logprob = teacher_wide - jax.nn.logsumexp(teacher_wide, axis=1, keepdims=True)
    student_logprob = student_logits - jax.nn.logsumexp(student_logits, axis=1, keepdims=True)
    student_prob = jnp.exp(student_logprob)
    log_ratio = student_logprob - teacher_logprob
    kl_div = jnp.sum(student_prob * log_ratio, axis=1)
    picked = jnp.take_along_axis(-log_ratio, token_ids[:, None], axis=1)[:, 0]
    logit_grad = (student_prob * (log_ratio - kl_div[:, None])).astype(jnp.bfloat16)
    return picked, kl_div, logit_grad
```

```python
import functools

import jax
import jax.numpy as jnp
from jax import lax
from jax.experimental import pallas as pl
from jax.experimental.pallas import tpu as pltpu
from jax.sharding import PartitionSpec as P

AXES = ("tv", "sv")
GROUPS = 2
SHIFTS = (0, 1, 3, 2)
TILE = 512
F32 = jnp.float32
BF16 = jnp.bfloat16


def place(t, s):
    return t // 4, (t // 2) % 2, t % 2, s // 4, s % 4


def moved(x, step):
    pairs = []
    for source in range(128):
        z, xh, c, xl, y = step(*place(source // 8, source % 8))
        target = ((z % 4) * 4 + (xh % 2) * 2 + c % 2) * 8 + (xl % 2) * 4 + y % 4
        pairs.append((source, target))
    return lax.ppermute(x, AXES, pairs)


def along_z(d):
    return lambda z, xh, c, xl, y: (z + d, xh, c, xl, y)


def along_y(d):
    return lambda z, xh, c, xl, y: (z, xh, c, xl, y + d)


def other_core(z, xh, c, xl, y):
    return z, xh, c + 1, xl, y


def other_xh(z, xh, c, xl, y):
    return z, xh + 1, c, xl, y


def other_xl(z, xh, c, xl, y):
    return z, xh, c, xl + 1, y


def ring(x, along):
    return [x if d == 0 else moved(x, along(d)) for d in SHIFTS]


def ordered(parts, here):
    back = jnp.stack([parts[SHIFTS.index(d)] for d in (3, 2, 1, 0)] * 2)
    return lax.dynamic_slice_in_dim(back, 3 - here, 4, axis=0)


def paired(x, step, here):
    other = moved(x, step)
    return jnp.where(here == 0, jnp.stack([x, other]), jnp.stack([other, x]))


def coded(x):
    top = jnp.maximum(jnp.max(jnp.abs(x), axis=1, keepdims=True), 1e-30)
    power = jnp.ceil(jnp.log2(top) + 1e-4)
    code = jnp.clip(jnp.round(x * jnp.exp2(15.0 - power)), -32767.0, 32767.0)
    return jnp.concatenate([code, power], axis=1).astype(jnp.int16)


def decoded(code):
    power = code[:, -1:].astype(F32)
    return code[:, :-1].astype(F32) * jnp.exp2(power - 15.0)


def student_kernel(hidden, w0, w1, w2, w3, theirs, ours, joint):
    depth = w0.shape[0]
    for k, w in enumerate((w0, w1, w2, w3)):
        joint[k * depth:(k + 1) * depth, :] = w[...]
    theirs[...] = jnp.dot(hidden[1], joint[...], preferred_element_type=F32)
    ours[...] = jnp.dot(hidden[0], joint[...], preferred_element_type=F32)


def student_partial(hidden, weights):
    _, rows, width = hidden.shape
    depth, words = weights[0].shape
    block = pl.BlockSpec((rows, TILE), lambda j: (0, j))
    return pl.pallas_call(
        student_kernel,
        grid=(pl.cdiv(words, TILE),),
        in_specs=[pl.BlockSpec((2, rows, width), lambda j: (0, 0, 0))]
        + [pl.BlockSpec((depth, TILE), lambda j: (0, j))] * 4,
        out_specs=[block, block],
        out_shape=[jax.ShapeDtypeStruct((rows, words), F32)] * 2,
        scratch_shapes=[pltpu.VMEM((4 * depth, TILE), BF16)],
        compiler_params=pltpu.CompilerParams(vmem_limit_bytes=40 << 20),
        cost_estimate=pl.CostEstimate(
            flops=4 * rows * width * words,
            bytes_accessed=2 * width * words + 8 * rows * words,
            transcendentals=0,
        ),
    )(hidden, *weights)


def teacher_kernel(hidden, weights, logits, total):
    k = pl.program_id(0)

    @pl.when(k == 0)
    def _():
        total[...] = jnp.zeros_like(total)

    total[...] += lax.dot_general(
        hidden[0], weights[0], (((1,), (1,)), ((), ())), preferred_element_type=F32
    )

    @pl.when(k == pl.num_programs(0) - 1)
    def _():
        logits[...] = total[...].astype(BF16)


def teacher_product(hidden, weights):
    steps, rows, depth = hidden.shape
    words = weights.shape[1]
    return pl.pallas_call(
        teacher_kernel,
        grid=(steps,),
        in_specs=[
            pl.BlockSpec((1, rows, depth), lambda k: (k, 0, 0)),
            pl.BlockSpec((1, words, depth), lambda k: (k, 0, 0)),
        ],
        out_specs=pl.BlockSpec((rows, words), lambda k: (0, 0)),
        out_shape=jax.ShapeDtypeStruct((rows, words), BF16),
        scratch_shapes=[pltpu.VMEM((rows, words), F32)],
        compiler_params=pltpu.CompilerParams(vmem_limit_bytes=40 << 20),
        cost_estimate=pl.CostEstimate(
            flops=2 * steps * rows * depth * words,
            bytes_accessed=2 * steps * depth * (rows + words) + 2 * rows * words,
            transcendentals=0,
        ),
    )(hidden, weights)


def student_rows(student_hidden, z, xh, c, xl, y):
    hidden = jnp.concatenate(ring(student_hidden, along_z), axis=1)
    hidden = ordered(ring(paired(hidden, other_xl, xl), along_y), y)
    rows = hidden.shape[2] // 2
    hidden = hidden.reshape(2, 2, 2, 2, rows, -1).transpose(3, 1, 2, 0, 4, 5)
    hidden = hidden.reshape(2, 2, 4, rows, -1)
    hidden = jnp.where(c == 0, hidden, hidden[::-1])
    hidden = jnp.where(xh == 0, hidden, hidden[:, ::-1])
    twice = jnp.concatenate([hidden, hidden], axis=2)
    hidden = lax.dynamic_slice_in_dim(twice, z, 4, axis=2)
    return hidden.reshape(2, 8 * rows, -1)


def student_weights(student_head, z):
    quarter = student_head.shape[1] // 4
    part = quarter // GROUPS
    groups = []
    for g in range(GROUPS):
        pieces = []
        for d in SHIFTS:
            start = ((z + d) % 4) * quarter + g * part
            pieces.append(lax.dynamic_slice_in_dim(student_head, start, part, axis=1))
        student_head, pieces = lax.optimization_barrier((student_head, pieces))
        groups.append([p if d == 0 else moved(p, along_z(d)) for d, p in zip(SHIFTS, pieces)])
    return groups


def student_logits(hidden, weights):
    theirs, ours = student_partial(hidden, weights)
    ours = ours + moved(theirs, other_core)
    half = ours.shape[0] // 2
    rows = half // 4
    full = ours[:half] + decoded(moved(coded(ours[half:]), other_xh))
    parts = []
    for d in SHIFTS:
        part = full[d * rows:(d + 1) * rows]
        parts.append(part if d == 0 else decoded(moved(coded(part), along_z(d))))
    return parts


def teacher_rows(teacher_hidden, z, xh, c, xl, y):
    hidden = paired(teacher_hidden, other_xh, xh)
    hidden = ordered(ring(hidden, along_z), z)
    hidden = paired(hidden, other_xl, xl)
    hidden = ordered(ring(hidden, along_y), y)
    hidden = paired(hidden, other_core, c)
    rows, depth = hidden.shape[5:]
    return hidden.transpose(2, 1, 3, 4, 0, 5, 6).reshape(8, 16 * rows, depth)


def teacher_logits(hidden, weights, z):
    logits = teacher_product(hidden, weights)
    rows, part = logits.shape[0] // 16, logits.shape[1]
    logits = lax.all_to_all(logits.reshape(16, rows, part), "tv", 0, 0, tiled=True)
    logits = lax.all_to_all(logits.reshape(8, 2, rows, part), "sv", 0, 0, tiled=True)
    logits = logits.reshape(2, GROUPS, 2, 2, rows, part).transpose(3, 0, 1, 4, 2, 5)
    logits = logits.reshape(4, GROUPS, rows, 2 * part)
    back = jnp.concatenate([logits[::-1]] * 2)
    return lax.dynamic_slice_in_dim(back, 3 - z, 4, axis=0)


def shards(teacher_hidden, student_hidden, teacher_head, student_head, token_ids):
    t, s = lax.axis_index("tv"), lax.axis_index("sv")
    here = place(t, s)
    z = here[0]
    width = student_head.shape[1]
    quarter = width // 4
    part = quarter // GROUPS
    words8 = teacher_head.shape[1] // 8
    s_hidden = student_rows(student_hidden, *here)
    s_weights = student_weights(student_head, z)
    pieces = jnp.stack([teacher_head[:, k * words8:(k + 1) * words8].T for k in range(8)])
    t_weights = lax.all_to_all(pieces, "sv", 0, 0, tiled=True)
    t_hidden = teacher_rows(teacher_hidden, *here)
    teacher = teacher_logits(t_hidden, t_weights, z).astype(F32)
    groups = [student_logits(s_hidden, weights) for weights in s_weights]
    student = jnp.stack(
        [jnp.stack([parts[SHIFTS.index(d)] for parts in groups]) for d in range(4)]
    )
    quarters = (z - jnp.arange(4)) % 4
    starts = s * width + quarters[:, None] * quarter + jnp.arange(GROUPS)[None, :] * part
    words = starts[:, :, None, None] + lax.broadcasted_iota(jnp.int32, student.shape, 3)
    gap = student - teacher
    picked = jnp.sum(jnp.where(words == token_ids[:, None], gap, 0.0), axis=(0, 1, 3))
    peak_s = jnp.max(student, axis=(0, 1, 3))
    peak_t = jnp.max(teacher, axis=(0, 1, 3))
    raw = jnp.exp(student - peak_s[:, None])
    mass_s = jnp.sum(raw, axis=(0, 1, 3))
    mass_t = jnp.sum(jnp.exp(teacher - peak_t[:, None]), axis=(0, 1, 3))
    cross = jnp.sum(raw * gap, axis=(0, 1, 3))
    stats = jnp.stack([peak_s, mass_s, cross, peak_t, mass_t, picked])
    stats = lax.all_gather(stats, "sv", axis=0)
    top_s = jnp.max(stats[:, 0], axis=0)
    top_t = jnp.max(stats[:, 3], axis=0)
    scale_s = jnp.exp(stats[:, 0] - top_s)
    scale_t = jnp.exp(stats[:, 3] - top_t)
    total_s = jnp.sum(stats[:, 1] * scale_s, axis=0)
    total_t = jnp.sum(stats[:, 4] * scale_t, axis=0)
    norm_s = top_s + jnp.log(total_s)
    norm_t = top_t + jnp.log(total_t)
    mean_gap = jnp.sum(stats[:, 2] * scale_s, axis=0) / total_s
    kl_div = mean_gap - norm_s + norm_t
    rewards = norm_s - norm_t - jnp.sum(stats[:, 5], axis=0)
    prob = jnp.exp(student - norm_s[:, None])
    grad = (prob * (gap - mean_gap[:, None])).astype(BF16)
    back = jnp.concatenate([grad[::-1]] * 2)
    grad = lax.dynamic_slice_in_dim(back, 3 - z, 4, axis=0)
    logit_grad = grad.transpose(2, 0, 1, 3).reshape(grad.shape[2], width)
    return rewards, kl_div, logit_grad


def solution(mesh):
    in_specs = (P("tv", "sv"), P("sv", "tv"), P("sv", "tv"), P("tv", "sv"), P("tv"))
    out_specs = (P("tv"), P("tv"), P("tv", "sv"))
    return jax.shard_map(shards, mesh=mesh, in_specs=in_specs, out_specs=out_specs, check_vma=False)
```

```python
import functools

import jax
import jax.numpy as jnp
from jax import lax
from jax.experimental import pallas as pl
from jax.experimental.pallas import tpu as pltpu
from jax.sharding import PartitionSpec as P

AXES = ("tv", "sv")
GROUPS = 2
SHIFTS = (0, 1, 3, 2)
TILE = 512
F32 = jnp.float32
BF16 = jnp.bfloat16


def place(t, s):
    return t // 4, (t // 2) % 2, t % 2, s // 4, s % 4


def moved(x, step):
    pairs = []
    for source in range(128):
        z, xh, c, xl, y = step(*place(source // 8, source % 8))
        target = ((z % 4) * 4 + (xh % 2) * 2 + c % 2) * 8 + (xl % 2) * 4 + y % 4
        pairs.append((source, target))
    return lax.ppermute(x, AXES, pairs)


def along_z(d):
    return lambda z, xh, c, xl, y: (z + d, xh, c, xl, y)


def along_y(d):
    return lambda z, xh, c, xl, y: (z, xh, c, xl, y + d)


def other_core(z, xh, c, xl, y):
    return z, xh, c + 1, xl, y


def other_xh(z, xh, c, xl, y):
    return z, xh + 1, c, xl, y


def other_xl(z, xh, c, xl, y):
    return z, xh, c, xl + 1, y


def ring(x, along):
    return [x if d == 0 else moved(x, along(d)) for d in SHIFTS]


def ordered(parts, here):
    back = jnp.stack([parts[SHIFTS.index(d)] for d in (3, 2, 1, 0)] * 2)
    return lax.dynamic_slice_in_dim(back, 3 - here, 4, axis=0)


def paired(x, step, here, axis=0):
    other = moved(x, step)
    return jnp.where(
        here == 0, jnp.stack([x, other], axis=axis), jnp.stack([other, x], axis=axis)
    )


def coded(x):
    top = jnp.maximum(jnp.max(jnp.abs(x), axis=1, keepdims=True), 1e-30)
    power = jnp.ceil(jnp.log2(top) + 1e-4)
    code = jnp.clip(jnp.round(x * jnp.exp2(15.0 - power)), -32767.0, 32767.0)
    column = lax.broadcasted_iota(jnp.int32, x.shape, 1)
    return jnp.where(column == x.shape[1] - 1, power, code).astype(jnp.int16)


def decoded(code):
    power = code[:, -1:].astype(F32)
    return code.astype(F32) * jnp.exp2(power - 15.0)


def student_kernel(words, hidden, w0, w1, w2, w3, theirs, ours, joint):
    depth = w0.shape[0]
    for k, w in enumerate((w0, w1, w2, w3)):
        joint[k * depth:(k + 1) * depth, :] = w[...]
    column = pl.program_id(0) * TILE + lax.broadcasted_iota(jnp.int32, ours.shape, 1)
    for part, out in ((1, theirs), (0, ours)):
        logits = jnp.dot(hidden[part], joint[...], preferred_element_type=F32)
        out[...] = jnp.where(column < words, logits, 0.0)


def student_partial(hidden, weights, padded):
    _, rows, width = hidden.shape
    depth, words = weights[0].shape
    block = pl.BlockSpec((rows, TILE), lambda j: (0, j))
    return pl.pallas_call(
        functools.partial(student_kernel, words),
        grid=(pl.cdiv(padded, TILE),),
        in_specs=[pl.BlockSpec((2, rows, width), lambda j: (0, 0, 0))]
        + [pl.BlockSpec((depth, TILE), lambda j: (0, j))] * 4,
        out_specs=[block, block],
        out_shape=[jax.ShapeDtypeStruct((rows, padded), F32)] * 2,
        scratch_shapes=[pltpu.VMEM((4 * depth, TILE), BF16)],
        compiler_params=pltpu.CompilerParams(vmem_limit_bytes=40 << 20),
        cost_estimate=pl.CostEstimate(
            flops=4 * rows * width * words,
            bytes_accessed=2 * width * words + 8 * rows * words,
            transcendentals=0,
        ),
    )(hidden, *weights)


def teacher_kernel(hidden, weights, logits, total):
    k = pl.program_id(0)

    @pl.when(k == 0)
    def _():
        total[...] = jnp.zeros_like(total)

    total[...] += lax.dot_general(
        hidden[0], weights[0], (((1,), (1,)), ((), ())), preferred_element_type=F32
    )

    @pl.when(k == pl.num_programs(0) - 1)
    def _():
        logits[...] = total[...].astype(BF16)


def teacher_product(hidden, weights):
    steps, rows, depth = hidden.shape
    words = weights.shape[1]
    return pl.pallas_call(
        teacher_kernel,
        grid=(steps,),
        in_specs=[
            pl.BlockSpec((1, rows, depth), lambda k: (k, 0, 0)),
            pl.BlockSpec((1, words, depth), lambda k: (k, 0, 0)),
        ],
        out_specs=pl.BlockSpec((rows, words), lambda k: (0, 0)),
        out_shape=jax.ShapeDtypeStruct((rows, words), BF16),
        scratch_shapes=[pltpu.VMEM((rows, words), F32)],
        compiler_params=pltpu.CompilerParams(vmem_limit_bytes=40 << 20),
        cost_estimate=pl.CostEstimate(
            flops=2 * steps * rows * depth * words,
            bytes_accessed=2 * steps * depth * (rows + words) + 2 * rows * words,
            transcendentals=0,
        ),
    )(hidden, weights)


def student_rows(hidden, z, xh, c):
    rows = hidden.shape[2] // 2
    hidden = hidden.reshape(2, 2, 2, 2, rows, -1).transpose(3, 1, 2, 0, 4, 5)
    hidden = hidden.reshape(2, 2, 4, rows, -1)
    hidden = jnp.where(c == 0, hidden, hidden[::-1])
    hidden = jnp.where(xh == 0, hidden, hidden[:, ::-1])
    twice = jnp.concatenate([hidden, hidden], axis=2)
    hidden = lax.dynamic_slice_in_dim(twice, z, 4, axis=2)
    return hidden.reshape(2, 8 * rows, -1)


def first_stage(teacher_hidden, student_hidden):
    width = teacher_hidden.shape[1]
    pack = jnp.concatenate([teacher_hidden, student_hidden.reshape(-1, width)])
    return ring(pack, along_z)


def all_rows(stage, teacher_shape, student_shape, z, xh, c, xl, y):
    rows, width = teacher_shape
    s_rows, s_depth = student_shape
    teacher = ordered([part[:rows] for part in stage], z)
    teacher = paired(teacher, other_xh, xh, axis=1)
    student = jnp.concatenate([part[rows:].reshape(s_rows, s_depth) for part in stage], axis=1)
    pack = jnp.concatenate([teacher.reshape(-1, width), student.reshape(-1, width)])
    pack = ordered(ring(paired(pack, other_xl, xl), along_y), y)
    student = pack[:, :, 8 * rows:].reshape(4, 2, s_rows, 4 * s_depth)
    teacher = pack[:, :, :8 * rows].transpose(1, 0, 2, 3).reshape(8, 8, rows, width)
    teacher = paired(teacher, other_core, c, axis=2)
    return teacher.reshape(8, 16 * rows, width), student_rows(student, z, xh, c)


def student_pieces(student_head, z, start, words):
    quarter = student_head.shape[1] // 4
    return [
        lax.dynamic_slice_in_dim(student_head, ((z + d) % 4) * quarter + start, words, axis=1)
        for d in SHIFTS
    ]


def sent(pieces):
    return [p if d == 0 else moved(p, along_z(d)) for d, p in zip(SHIFTS, pieces)]


def student_logits(hidden, weights, padded):
    theirs, ours = student_partial(hidden, weights, padded)
    ours = ours + moved(theirs, other_core)
    half = ours.shape[0] // 2
    rows = half // 4
    full = ours[:half] + decoded(moved(coded(ours[half:]), other_xh))
    parts = []
    for d in SHIFTS:
        part = full[d * rows:(d + 1) * rows]
        parts.append(part if d == 0 else decoded(moved(coded(part), along_z(d))))
    return parts


def teacher_logits(hidden, weights, padded):
    logits = teacher_product(hidden, weights)
    rows, part = logits.shape[0] // 16, logits.shape[1]
    logits = lax.all_to_all(logits.reshape(16, rows, part), "tv", 0, 0, tiled=True)
    logits = lax.all_to_all(logits.reshape(8, 2, rows, part), "sv", 0, 0, tiled=True)
    logits = logits.reshape(GROUPS, 4, 2, rows, part).transpose(2, 0, 3, 1, 4)
    logits = logits.reshape(2, GROUPS, rows, 4 * part)
    return jnp.pad(logits, ((0, 0), (0, 0), (0, 0), (0, padded - 4 * part)))


def pooled(a, b):
    top_s = jnp.maximum(a[0], b[0])
    top_t = jnp.maximum(a[3], b[3])
    a_s, b_s = jnp.exp(a[0] - top_s), jnp.exp(b[0] - top_s)
    a_t, b_t = jnp.exp(a[3] - top_t), jnp.exp(b[3] - top_t)
    return jnp.stack([
        top_s,
        a[1] * a_s + b[1] * b_s,
        a[2] * a_s + b[2] * b_s,
        top_t,
        a[4] * a_t + b[4] * b_t,
        a[5] + b[5],
    ])


def shards(teacher_hidden, student_hidden, teacher_head, student_head, token_ids):
    t, s = lax.axis_index("tv"), lax.axis_index("sv")
    here = place(t, s)
    z, c = here[0], here[2]
    width = student_head.shape[1]
    quarter = width // 4
    chunk = -(-quarter // 64) * 8
    sizes = (4 * chunk, quarter - 4 * chunk)
    padded = (4 * chunk // 128 + 1) * 128
    stage = first_stage(teacher_hidden, student_hidden)
    tall = teacher_head.T
    t_first = tall[:8 * chunk].reshape(8, chunk, -1)
    t_second = jnp.pad(tall[quarter:], ((0, 8 * chunk - quarter), (0, 0))).reshape(8, chunk, -1)
    student_head, stage, t_first = lax.optimization_barrier((student_head, stage, t_first))
    s_first = student_pieces(student_head, z, 0, sizes[0])
    t_first = lax.all_to_all(t_first, "sv", 0, 0, tiled=True)
    s_first = sent(s_first)
    t_hidden, s_hidden = all_rows(stage, teacher_hidden.shape, student_hidden.shape, *here)
    s_second = student_pieces(student_head, z, sizes[0], sizes[1])
    s_second, t_second, t_first = lax.optimization_barrier((s_second, t_second, t_first))
    t_second = lax.all_to_all(t_second, "sv", 0, 0, tiled=True)
    s_second = sent(s_second)
    s_second, t_second = lax.optimization_barrier((s_second, t_second))
    teacher = [teacher_logits(t_hidden, w, padded) for w in (t_first, t_second)]
    teacher = jnp.stack(teacher, axis=1).reshape(4, GROUPS, -1, padded).astype(F32)
    groups = [student_logits(s_hidden, w, padded) for w in (s_first, s_second)]
    student = jnp.zeros(teacher.shape, F32)
    for g, parts in enumerate(groups):
        for d, part in zip(SHIFTS, parts):
            student = lax.dynamic_update_slice(student, part[None, None], ((z - d) % 4, g, 0, 0))
    column = lax.broadcasted_iota(jnp.int32, student.shape, 3)
    group = lax.broadcasted_iota(jnp.int32, student.shape, 1)
    index = lax.broadcasted_iota(jnp.int32, student.shape, 0) * quarter + group * sizes[0] + column
    real = column < jnp.where(group == 0, sizes[0], sizes[1])
    student = jnp.where(real, student, -1e30)
    teacher = jnp.where(real, teacher, -1e30)
    gap = student - teacher
    chosen = real & (s * width + index == token_ids[:, None])
    picked = jnp.sum(jnp.where(chosen, gap, 0.0), axis=(0, 1, 3))
    peak_s = jnp.max(student, axis=(0, 1, 3))
    peak_t = jnp.max(teacher, axis=(0, 1, 3))
    raw = jnp.exp(student - peak_s[:, None])
    mass_s = jnp.sum(raw, axis=(0, 1, 3))
    mass_t = jnp.sum(jnp.exp(teacher - peak_t[:, None]), axis=(0, 1, 3))
    cross = jnp.sum(raw * gap, axis=(0, 1, 3))
    stats = jnp.stack([peak_s, mass_s, cross, peak_t, mass_t, picked])
    stats = pooled(stats, moved(stats, other_xl))
    stats = functools.reduce(pooled, ring(stats, along_y))
    norm_s = stats[0] + jnp.log(stats[1])
    norm_t = stats[3] + jnp.log(stats[4])
    mean_gap = stats[2] / stats[1]
    kl_div = mean_gap - norm_s + norm_t
    rewards = norm_s - norm_t - stats[5]
    prob = jnp.exp(student - norm_s[:, None])
    grad = (prob * (gap - mean_gap[:, None])).astype(BF16)
    pieces = [grad[q, g, :, :sizes[g]] for q in range(4) for g in range(GROUPS)]
    return rewards, kl_div, jnp.concatenate(pieces, axis=1)


def solution(mesh):
    in_specs = (P("tv", "sv"), P("sv", "tv"), P("sv", "tv"), P("tv", "sv"), P("tv"))
    out_specs = (P("tv"), P("tv"), P("tv", "sv"))
    return jax.shard_map(shards, mesh=mesh, in_specs=in_specs, out_specs=out_specs, check_vma=False)
```

```python
import functools

import jax
import jax.numpy as jnp
from jax import lax
from jax.experimental import pallas as pl
from jax.experimental.pallas import tpu as pltpu
from jax.sharding import PartitionSpec as P

AXES = ("tv", "sv")
GROUPS = 2
SHIFTS = (0, 1, 3, 2)
TILE = 512
F32 = jnp.float32
BF16 = jnp.bfloat16


def place(t, s):
    return t // 4, (t // 2) % 2, t % 2, s // 4, s % 4


def moved(x, step):
    pairs = []
    for source in range(128):
        z, xh, c, xl, y = step(*place(source // 8, source % 8))
        target = ((z % 4) * 4 + (xh % 2) * 2 + c % 2) * 8 + (xl % 2) * 4 + y % 4
        pairs.append((source, target))
    return lax.ppermute(x, AXES, pairs)


def along_z(d):
    return lambda z, xh, c, xl, y: (z + d, xh, c, xl, y)


def along_y(d):
    return lambda z, xh, c, xl, y: (z, xh, c, xl, y + d)


def other_core(z, xh, c, xl, y):
    return z, xh, c + 1, xl, y


def other_xh(z, xh, c, xl, y):
    return z, xh + 1, c, xl, y


def other_xl(z, xh, c, xl, y):
    return z, xh, c, xl + 1, y


def ring(x, along):
    return [x if d == 0 else moved(x, along(d)) for d in SHIFTS]


def ordered(parts, here):
    back = jnp.stack([parts[SHIFTS.index(d)] for d in (3, 2, 1, 0)] * 2)
    return lax.dynamic_slice_in_dim(back, 3 - here, 4, axis=0)


def paired(x, step, here, axis=0):
    other = moved(x, step)
    return jnp.where(
        here == 0, jnp.stack([x, other], axis=axis), jnp.stack([other, x], axis=axis)
    )


def coded(x):
    top = jnp.maximum(jnp.max(jnp.abs(x), axis=1, keepdims=True), 1e-30)
    power = jnp.ceil(jnp.log2(top) + 1e-4)
    code = jnp.clip(jnp.round(x * jnp.exp2(15.0 - power)), -32767.0, 32767.0)
    column = lax.broadcasted_iota(jnp.int32, x.shape, 1)
    return jnp.where(column == x.shape[1] - 1, power, code).astype(jnp.int16)


def decoded(code):
    power = code[:, -1:].astype(F32)
    return code.astype(F32) * jnp.exp2(power - 15.0)


def student_kernel(words, hidden, w0, w1, w2, w3, theirs, ours, joint):
    depth = w0.shape[0]
    for k, w in enumerate((w0, w1, w2, w3)):
        joint[k * depth:(k + 1) * depth, :] = w[...]
    column = pl.program_id(0) * TILE + lax.broadcasted_iota(jnp.int32, ours.shape, 1)
    for part, out in ((1, theirs), (0, ours)):
        logits = jnp.dot(hidden[part], joint[...], preferred_element_type=F32)
        out[...] = jnp.where(column < words, logits, 0.0)


def student_partial(hidden, weights, padded):
    _, rows, width = hidden.shape
    depth, words = weights[0].shape
    block = pl.BlockSpec((rows, TILE), lambda j: (0, j))
    return pl.pallas_call(
        functools.partial(student_kernel, words),
        grid=(pl.cdiv(padded, TILE),),
        in_specs=[pl.BlockSpec((2, rows, width), lambda j: (0, 0, 0))]
        + [pl.BlockSpec((depth, TILE), lambda j: (0, j))] * 4,
        out_specs=[block, block],
        out_shape=[jax.ShapeDtypeStruct((rows, padded), F32)] * 2,
        scratch_shapes=[pltpu.VMEM((4 * depth, TILE), BF16)],
        compiler_params=pltpu.CompilerParams(vmem_limit_bytes=40 << 20),
        cost_estimate=pl.CostEstimate(
            flops=4 * rows * width * words,
            bytes_accessed=2 * width * words + 8 * rows * words,
            transcendentals=0,
        ),
    )(hidden, *weights)


def teacher_kernel(words, here, hidden, weights, theirs, ours, total):
    half, k = pl.program_id(0), pl.program_id(1)

    @pl.when(k == 0)
    def _():
        total[...] = jnp.zeros_like(total)

    total[:, :words] += lax.dot_general(
        hidden[0], weights[0], (((1,), (1,)), ((), ())), preferred_element_type=F32
    )

    @pl.when((k == pl.num_programs(1) - 1) & (half == 0))
    def _():
        theirs[...] = total[...]

    @pl.when((k == pl.num_programs(1) - 1) & (half == 1))
    def _():
        ours[...] = total[...]


def teacher_partial(hidden, weights, xl, padded):
    steps, rows, depth = hidden.shape
    words = weights.shape[1] // 2
    block = pl.BlockSpec((rows, padded), lambda h, k, here: (0, 0))
    return pl.pallas_call(
        functools.partial(teacher_kernel, words),
        grid_spec=pltpu.PrefetchScalarGridSpec(
            num_scalar_prefetch=1,
            grid=(2, steps),
            in_specs=[
                pl.BlockSpec((1, rows, depth), lambda h, k, here: (k, 0, 0)),
                pl.BlockSpec((1, words, depth), lambda h, k, here: (k, (h + here[0] + 1) % 2, 0)),
            ],
            out_specs=[block, block],
            scratch_shapes=[pltpu.VMEM((rows, padded), F32)],
        ),
        out_shape=[jax.ShapeDtypeStruct((rows, padded), F32)] * 2,
        compiler_params=pltpu.CompilerParams(vmem_limit_bytes=40 << 20),
        cost_estimate=pl.CostEstimate(
            flops=4 * steps * rows * depth * words,
            bytes_accessed=2 * steps * depth * 2 * (rows + words) + 8 * rows * padded,
            transcendentals=0,
        ),
    )(xl.reshape(1).astype(jnp.int32), hidden, weights)


def student_rows(hidden, z, xh, c):
    rows = hidden.shape[2] // 2
    hidden = hidden.reshape(2, 2, 2, 2, rows, -1).transpose(3, 1, 2, 0, 4, 5)
    hidden = hidden.reshape(2, 2, 4, rows, -1)
    hidden = jnp.where(c == 0, hidden, hidden[::-1])
    hidden = jnp.where(xh == 0, hidden, hidden[:, ::-1])
    twice = jnp.concatenate([hidden, hidden], axis=2)
    hidden = lax.dynamic_slice_in_dim(twice, z, 4, axis=2)
    return hidden.reshape(2, 8 * rows, -1)


def first_stage(teacher_hidden, student_hidden):
    width = teacher_hidden.shape[1]
    pack = jnp.concatenate([teacher_hidden, student_hidden.reshape(-1, width)])
    return ring(pack, along_z)


def all_rows(stage, teacher_shape, student_shape, z, xh, c, xl, y):
    rows, width = teacher_shape
    s_rows, s_depth = student_shape
    student = jnp.concatenate([part[rows:].reshape(s_rows, s_depth) for part in stage], axis=1)
    student = paired(student, other_xl, xl)
    teacher = ordered(ring(ordered([part[:rows] for part in stage], z), along_y), y)
    student = ordered(ring(student, along_y), y)
    teacher = paired(teacher.reshape(16, rows, width), other_xh, xh, axis=1)
    teacher = paired(teacher.reshape(32, rows, width), other_core, c, axis=1)
    return teacher.reshape(4, 16 * rows, width), student_rows(student, z, xh, c)


def student_pieces(student_head, z, start, words):
    quarter = student_head.shape[1] // 4
    return [
        lax.dynamic_slice_in_dim(student_head, ((z + d) % 4) * quarter + start, words, axis=1)
        for d in SHIFTS
    ]


def sent(pieces):
    return [p if d == 0 else moved(p, along_z(d)) for d, p in zip(SHIFTS, pieces)]


def student_halves(hidden, weights, padded):
    theirs, ours = student_partial(hidden, weights, padded)
    ours = ours + moved(theirs, other_core)
    half = ours.shape[0] // 2
    return ours[:half], moved(coded(ours[half:]), other_xh)


def student_logits(ours, theirs):
    full = ours + decoded(theirs)
    rows = full.shape[0] // 4
    parts = [full[k * rows:(k + 1) * rows] for k in range(4)]
    return [parts[0]] + [moved(coded(parts[d]), along_z(d)) for d in SHIFTS[1:]]


def teacher_logits(ours, theirs):
    return (ours + decoded(theirs)).astype(BF16)


def teacher_place(logits, chunk, padded):
    rows, part = logits.shape[0] // 16, logits.shape[1]
    logits = lax.all_to_all(logits.reshape(16, rows, part), "tv", 0, 0, tiled=True)
    logits = lax.all_to_all(logits.reshape(8, 2, rows, part), "sv", 0, 0, tiled=True)
    logits = logits.reshape(2, GROUPS, 2, 2, rows, part)[..., :chunk].transpose(3, 1, 4, 2, 0, 5)
    logits = logits.reshape(2, GROUPS, rows, 4 * chunk)
    return jnp.pad(logits, ((0, 0), (0, 0), (0, 0), (0, padded - 4 * chunk)))


def tiled_rows(rows, chunk):
    rows = rows.reshape(4, 2, chunk, -1)
    rows = jnp.pad(rows, ((0, 0), (0, 0), (0, -chunk % 16), (0, 0)))
    return rows.reshape(4, 2 * rows.shape[2], -1)


def over_y(pieces):
    groups = [[0, 1, 2, 3], [4, 5, 6, 7]]
    return lax.all_to_all(pieces, "sv", 0, 0, axis_index_groups=groups, tiled=True)


def pooled(a, b):
    top_s = jnp.maximum(a[0], b[0])
    top_t = jnp.maximum(a[3], b[3])
    a_s, b_s = jnp.exp(a[0] - top_s), jnp.exp(b[0] - top_s)
    a_t, b_t = jnp.exp(a[3] - top_t), jnp.exp(b[3] - top_t)
    return jnp.stack([
        top_s,
        a[1] * a_s + b[1] * b_s,
        a[2] * a_s + b[2] * b_s,
        top_t,
        a[4] * a_t + b[4] * b_t,
        a[5] + b[5],
    ])


def shards(teacher_hidden, student_hidden, teacher_head, student_head, token_ids):
    t, s = lax.axis_index("tv"), lax.axis_index("sv")
    here = place(t, s)
    z, c = here[0], here[2]
    width = student_head.shape[1]
    quarter = width // 4
    chunk = -(-quarter // 64) * 8
    sizes = (4 * chunk, quarter - 4 * chunk)
    padded = (4 * chunk // 128 + 1) * 128
    t_padded = (chunk // 128 + 1) * 128
    barrier = lax.optimization_barrier
    xl = here[3]

    stage = first_stage(teacher_hidden, student_hidden)
    tall = teacher_head.T
    t_first = tiled_rows(tall[:8 * chunk], chunk)
    s_first = student_pieces(student_head, z, 0, sizes[0])
    stage, t_first, s_first = barrier((stage, t_first, s_first))
    s_first = sent(s_first)
    t_first = over_y(t_first)
    t_hidden, s_hidden = all_rows(stage, teacher_hidden.shape, student_hidden.shape, *here)

    t_second = jnp.pad(tall[quarter:], ((0, 8 * chunk - quarter), (0, 0)))
    t_second = tiled_rows(t_second, chunk)
    s_second = student_pieces(student_head, z, sizes[0], sizes[1])
    s_second, t_second, s_first, t_first, t_hidden, s_hidden = barrier(
        (s_second, t_second, s_first, t_first, t_hidden, s_hidden)
    )
    s_second = sent(s_second)
    t_second = over_y(t_second)
    t_theirs, t_ours = teacher_partial(t_hidden, t_first, xl, t_padded)
    t_first = t_ours, moved(coded(t_theirs), other_xl)
    s_first = student_halves(s_hidden, s_first, padded)

    s_second, t_second, t_first, s_first = barrier((s_second, t_second, t_first, s_first))
    t_theirs, t_ours = teacher_partial(t_hidden, t_second, xl, t_padded)
    t_theirs, t_ours, s_second = barrier((t_theirs, t_ours, s_second))
    t_second = t_ours, moved(coded(t_theirs), other_xl)
    t_first = teacher_place(teacher_logits(*t_first), chunk, padded)
    s_first = student_logits(*s_first)
    s_second = student_halves(s_hidden, s_second, padded)
    t_second, t_first, s_first, s_second = barrier((t_second, t_first, s_first, s_second))
    t_second = teacher_place(teacher_logits(*t_second), chunk, padded)
    s_second = student_logits(*s_second)

    teacher = jnp.stack([t_first, t_second], axis=1).reshape(4, GROUPS, -1, padded).astype(F32)
    student = jnp.zeros(teacher.shape, F32)
    for g, parts in enumerate((s_first, s_second)):
        for d, part in zip(SHIFTS, parts):
            part = part if d == 0 else decoded(part)
            student = lax.dynamic_update_slice(student, part[None, None], ((z - d) % 4, g, 0, 0))
    column = lax.broadcasted_iota(jnp.int32, student.shape, 3)
    group = lax.broadcasted_iota(jnp.int32, student.shape, 1)
    index = lax.broadcasted_iota(jnp.int32, student.shape, 0) * quarter + group * sizes[0] + column
    real = column < jnp.where(group == 0, sizes[0], sizes[1])
    student = jnp.where(real, student, -1e30)
    teacher = jnp.where(real, teacher, -1e30)
    gap = student - teacher
    chosen = real & (s * width + index == token_ids[:, None])
    picked = jnp.sum(jnp.where(chosen, gap, 0.0), axis=(0, 1, 3))
    peak_s = jnp.max(student, axis=(0, 1, 3))
    peak_t = jnp.max(teacher, axis=(0, 1, 3))
    raw = jnp.exp(student - peak_s[:, None])
    mass_s = jnp.sum(raw, axis=(0, 1, 3))
    mass_t = jnp.sum(jnp.exp(teacher - peak_t[:, None]), axis=(0, 1, 3))
    cross = jnp.sum(raw * gap, axis=(0, 1, 3))
    stats = jnp.stack([peak_s, mass_s, cross, peak_t, mass_t, picked])
    stats = pooled(stats, moved(stats, other_xl))
    stats = functools.reduce(pooled, ring(stats, along_y))
    norm_s = stats[0] + jnp.log(stats[1])
    norm_t = stats[3] + jnp.log(stats[4])
    mean_gap = stats[2] / stats[1]
    kl_div = mean_gap - norm_s + norm_t
    rewards = norm_s - norm_t - stats[5]
    prob = jnp.exp(student - norm_s[:, None])
    grad = (prob * (gap - mean_gap[:, None])).astype(BF16)
    pieces = [grad[q, g, :, :sizes[g]] for q in range(4) for g in range(GROUPS)]
    return rewards, kl_div, jnp.concatenate(pieces, axis=1)


def solution(mesh):
    in_specs = (P("tv", "sv"), P("sv", "tv"), P("sv", "tv"), P("tv", "sv"), P("tv"))
    out_specs = (P("tv"), P("tv"), P("tv", "sv"))
    return jax.shard_map(shards, mesh=mesh, in_specs=in_specs, out_specs=out_specs, check_vma=False)
```

```python
import functools

import jax
import jax.numpy as jnp
from jax import lax
from jax.experimental import pallas as pl
from jax.experimental.pallas import tpu as pltpu
from jax.sharding import PartitionSpec as P

AXES = ("tv", "sv")
SHIFTS = (0, 1, 3, 2)
TILE = 256
F32 = jnp.float32
BF16 = jnp.bfloat16


def place(t, s):
    return t // 4, (t // 2) % 2, t % 2, s // 4, s % 4


def moved(x, step):
    pairs = []
    for source in range(128):
        z, xh, c, xl, y = step(*place(source // 8, source % 8))
        target = ((z % 4) * 4 + (xh % 2) * 2 + c % 2) * 8 + (xl % 2) * 4 + y % 4
        pairs.append((source, target))
    return lax.ppermute(x, AXES, pairs)


def along_z(d):
    return lambda z, xh, c, xl, y: (z + d, xh, c, xl, y)


def along_y(d):
    return lambda z, xh, c, xl, y: (z, xh, c, xl, y + d)


def other_core(z, xh, c, xl, y):
    return z, xh, c + 1, xl, y


def other_xh(z, xh, c, xl, y):
    return z, xh + 1, c, xl, y


def other_xl(z, xh, c, xl, y):
    return z, xh, c, xl + 1, y


def ring(x, along):
    return [x if d == 0 else moved(x, along(d)) for d in SHIFTS]


def ordered(parts, here):
    back = jnp.stack([parts[SHIFTS.index(d)] for d in (3, 2, 1, 0)] * 2)
    return lax.dynamic_slice_in_dim(back, 3 - here, 4, axis=0)


def paired(x, step, here, axis=0):
    other = moved(x, step)
    return jnp.where(
        here == 0, jnp.stack([x, other], axis=axis), jnp.stack([other, x], axis=axis)
    )


def coded(x):
    top = jnp.maximum(jnp.max(jnp.abs(x), axis=1, keepdims=True), 1e-30)
    power = jnp.ceil(jnp.log2(top) + 1e-4)
    code = jnp.clip(jnp.round(x * jnp.exp2(15.0 - power)), -32767.0, 32767.0)
    column = lax.broadcasted_iota(jnp.int32, x.shape, 1)
    return jnp.where(column == x.shape[1] - 1, power, code).astype(jnp.int16)


def decoded(code):
    power = code[:, -1:].astype(F32)
    return code.astype(F32) * jnp.exp2(power - 15.0)


def student_kernel(words, hidden, w0, w1, w2, w3, theirs, ours, joint):
    depth = w0.shape[0]
    for k, w in enumerate((w0, w1, w2, w3)):
        joint[k * depth:(k + 1) * depth, :] = w[...]
    column = pl.program_id(0) * TILE + lax.broadcasted_iota(jnp.int32, ours.shape, 1)
    for part, out in ((1, theirs), (0, ours)):
        logits = jnp.dot(hidden[part], joint[...], preferred_element_type=F32)
        out[...] = jnp.where(column < words, logits, 0.0)


def student_partial(hidden, weights, first, words):
    _, rows, width = hidden.shape
    depth = weights[0].shape[0]
    padded = (words // 128 + 1) * 128
    last = pl.cdiv(weights[0].shape[1], TILE) - 1
    block = pl.BlockSpec((rows, TILE), lambda j: (0, j))
    return pl.pallas_call(
        functools.partial(student_kernel, words),
        grid=(pl.cdiv(padded, TILE),),
        in_specs=[pl.BlockSpec((2, rows, width), lambda j: (0, 0, 0))]
        + [pl.BlockSpec((depth, TILE), lambda j: (0, jnp.minimum(j + first, last)))] * 4,
        out_specs=[block, block],
        out_shape=[jax.ShapeDtypeStruct((rows, padded), F32)] * 2,
        scratch_shapes=[pltpu.VMEM((4 * depth, TILE), BF16)],
        compiler_params=pltpu.CompilerParams(vmem_limit_bytes=40 << 20),
        cost_estimate=pl.CostEstimate(
            flops=4 * rows * width * words,
            bytes_accessed=2 * width * words + 8 * rows * words,
            transcendentals=0,
        ),
    )(hidden, *weights)


def teacher_kernel(words, here, hidden, weights, theirs, ours, total):
    half, k = pl.program_id(0), pl.program_id(1)

    @pl.when(k == 0)
    def _():
        total[...] = jnp.zeros_like(total)

    total[:, :words] += lax.dot_general(
        hidden[0], weights[0], (((1,), (1,)), ((), ())), preferred_element_type=F32
    )

    @pl.when((k == pl.num_programs(1) - 1) & (half == 0))
    def _():
        theirs[...] = total[...]

    @pl.when((k == pl.num_programs(1) - 1) & (half == 1))
    def _():
        ours[...] = total[...]


def teacher_partial(hidden, weights, xl, padded):
    steps, rows, depth = hidden.shape
    words = weights.shape[1] // 2
    block = pl.BlockSpec((rows, padded), lambda h, k, here: (0, 0))
    return pl.pallas_call(
        functools.partial(teacher_kernel, words),
        grid_spec=pltpu.PrefetchScalarGridSpec(
            num_scalar_prefetch=1,
            grid=(2, steps),
            in_specs=[
                pl.BlockSpec((1, rows, depth), lambda h, k, here: (k, 0, 0)),
                pl.BlockSpec((1, words, depth), lambda h, k, here: (k, (h + here[0] + 1) % 2, 0)),
            ],
            out_specs=[block, block],
            scratch_shapes=[pltpu.VMEM((rows, padded), F32)],
        ),
        out_shape=[jax.ShapeDtypeStruct((rows, padded), F32)] * 2,
        compiler_params=pltpu.CompilerParams(vmem_limit_bytes=40 << 20),
        cost_estimate=pl.CostEstimate(
            flops=4 * steps * rows * depth * words,
            bytes_accessed=2 * steps * depth * 2 * (rows + words) + 8 * rows * padded,
            transcendentals=0,
        ),
    )(xl.reshape(1).astype(jnp.int32), hidden, weights)


def student_rows(hidden, z, xh, c):
    rows = hidden.shape[2] // 2
    hidden = hidden.reshape(2, 2, 2, 2, rows, -1).transpose(3, 1, 2, 0, 4, 5)
    hidden = hidden.reshape(2, 2, 4, rows, -1)
    hidden = jnp.where(c == 0, hidden, hidden[::-1])
    hidden = jnp.where(xh == 0, hidden, hidden[:, ::-1])
    twice = jnp.concatenate([hidden, hidden], axis=2)
    hidden = lax.dynamic_slice_in_dim(twice, z, 4, axis=2)
    return hidden.reshape(2, 8 * rows, -1)


def student_pieces(student_head, z):
    quarter = student_head.shape[1] // 4
    return [
        lax.dynamic_slice_in_dim(student_head, ((z + d) % 4) * quarter, quarter, axis=1)
        for d in SHIFTS
    ]


def sent(pieces):
    return [p if d == 0 else moved(p, along_z(d)) for d, p in zip(SHIFTS, pieces)]


def student_halves(hidden, weights, first, words):
    theirs, ours = student_partial(hidden, weights, first, words)
    ours = ours + moved(theirs, other_core)
    half = ours.shape[0] // 2
    return ours[:half], moved(coded(ours[half:]), other_xh)


def student_logits(ours, theirs):
    full = ours + decoded(theirs)
    rows = full.shape[0] // 4
    parts = [full[k * rows:(k + 1) * rows] for k in range(4)]
    return [parts[0]] + [moved(coded(parts[d]), along_z(d)) for d in SHIFTS[1:]]


def teacher_logits(ours, theirs):
    return (ours + decoded(theirs)).astype(BF16)


def teacher_place(logits, chunk):
    rows, part = logits.shape[0] // 16, logits.shape[1]
    logits = lax.all_to_all(logits.reshape(16, rows, part), "tv", 0, 0, tiled=True)
    logits = lax.all_to_all(logits.reshape(8, 2, rows, part), "sv", 0, 0, tiled=True)
    logits = logits.reshape(2, 4, 2, rows, part)[..., :chunk].transpose(2, 3, 1, 0, 4)
    return logits.reshape(2, rows, 8 * chunk)


def tiled_rows(rows, chunk):
    rows = rows.reshape(4, 2, chunk, -1)
    rows = jnp.pad(rows, ((0, 0), (0, 0), (0, -chunk % 16), (0, 0)))
    return rows.reshape(4, 2 * rows.shape[2], -1)


def over_y(pieces):
    groups = [[0, 1, 2, 3], [4, 5, 6, 7]]
    return lax.all_to_all(pieces, "sv", 0, 0, axis_index_groups=groups, tiled=True)


def pooled(a, b):
    top_s = jnp.maximum(a[0], b[0])
    top_t = jnp.maximum(a[3], b[3])
    a_s, b_s = jnp.exp(a[0] - top_s), jnp.exp(b[0] - top_s)
    a_t, b_t = jnp.exp(a[3] - top_t), jnp.exp(b[3] - top_t)
    return jnp.stack([
        top_s,
        a[1] * a_s + b[1] * b_s,
        a[2] * a_s + b[2] * b_s,
        top_t,
        a[4] * a_t + b[4] * b_t,
        a[5] + b[5],
    ])


def shards(teacher_hidden, student_hidden, teacher_head, student_head, token_ids):
    t, s = lax.axis_index("tv"), lax.axis_index("sv")
    z, xh, c, xl, y = place(t, s)
    width = student_head.shape[1]
    quarter = width // 4
    chunk = -(-quarter // 64) * 8
    t_padded = (chunk // 128 + 1) * 128
    padded = -(-8 * chunk // 128) * 128
    split = -(-quarter // (2 * TILE))
    sizes = (split * TILE, quarter - split * TILE)
    rows, depth = teacher_hidden.shape
    barrier = lax.optimization_barrier

    t_hidden = ring(teacher_hidden, along_y)
    s_hidden = ring(student_hidden, along_z)
    s_pieces = student_pieces(student_head, z)
    tall = teacher_head.T
    t_first = tiled_rows(tall[:8 * chunk], chunk)
    t_hidden = ordered(ring(ordered(t_hidden, y), along_z), z)
    s_hidden = paired(jnp.concatenate(s_hidden, axis=1), other_xl, xl)
    t_hidden, s_hidden, s_pieces, t_first = barrier((t_hidden, s_hidden, s_pieces, t_first))

    s_weights = sent(s_pieces)
    t_first = over_y(t_first)
    t_hidden = t_hidden.transpose(1, 0, 2, 3).reshape(16, rows, depth)
    t_hidden = paired(t_hidden, other_xh, xh, axis=1)
    t_hidden, tall = barrier((t_hidden, tall))
    t_hidden = paired(t_hidden.reshape(32, rows, depth), other_core, c, axis=1)
    t_hidden = t_hidden.reshape(4, 16 * rows, depth)
    t_second = jnp.pad(tall[quarter:], ((0, 8 * chunk - quarter), (0, 0)))
    t_second = tiled_rows(t_second, chunk)
    s_hidden, t_first = barrier((s_hidden, t_first))
    s_hidden = over_y(jnp.broadcast_to(s_hidden[None], (4,) + s_hidden.shape))
    t_second, s_hidden = barrier((t_second, s_hidden))
    t_second = over_y(t_second)
    s_hidden = student_rows(s_hidden, z, xh, c)
    t_theirs, t_ours = teacher_partial(t_hidden, t_first, xl, t_padded)
    t_first = t_ours, moved(coded(t_theirs), other_xl)

    t_second, t_first, s_hidden = barrier((t_second, t_first, s_hidden))
    t_theirs, t_ours = teacher_partial(t_hidden, t_second, xl, t_padded)
    t_theirs, t_ours, s_weights, t_first = barrier((t_theirs, t_ours, s_weights, t_first))
    t_second = t_ours, moved(coded(t_theirs), other_xl)
    t_first = teacher_place(teacher_logits(*t_first), chunk)
    s_first = student_halves(s_hidden, s_weights, 0, sizes[0])
    s_second = student_halves(s_hidden, s_weights, split, sizes[1])
    s_first = student_logits(*s_first)
    t_second, t_first = barrier((t_second, t_first))
    t_second = teacher_place(teacher_logits(*t_second), chunk)
    s_second = student_logits(*s_second)

    teacher = jnp.stack([t_first, t_second], axis=1).reshape(4, rows, 8 * chunk)
    teacher = jnp.pad(teacher, ((0, 0), (0, 0), (0, padded - 8 * chunk))).astype(F32)
    student = jnp.zeros(teacher.shape, F32)
    for start, parts in ((0, s_first), (sizes[0], s_second)):
        for d, part in zip(SHIFTS, parts):
            part = part if d == 0 else decoded(part)
            part = part[:, :min(part.shape[1], sizes[0] if start == 0 else padded - start)]
            student = lax.dynamic_update_slice(student, part[None], ((z - d) % 4, 0, start))
    column = lax.broadcasted_iota(jnp.int32, student.shape, 2)
    index = lax.broadcasted_iota(jnp.int32, student.shape, 0) * quarter + column
    real = column < quarter
    student = jnp.where(real, student, -1e30)
    teacher = jnp.where(real, teacher, -1e30)
    gap = student - teacher
    chosen = real & (s * width + index == token_ids[:, None])
    picked = jnp.sum(jnp.where(chosen, gap, 0.0), axis=(0, 2))
    peak_s = jnp.max(student, axis=(0, 2))
    peak_t = jnp.max(teacher, axis=(0, 2))
    raw = jnp.exp(student - peak_s[:, None])
    mass_s = jnp.sum(raw, axis=(0, 2))
    mass_t = jnp.sum(jnp.exp(teacher - peak_t[:, None]), axis=(0, 2))
    cross = jnp.sum(raw * gap, axis=(0, 2))
    stats = jnp.stack([peak_s, mass_s, cross, peak_t, mass_t, picked])
    stats = pooled(stats, moved(stats, other_xl))
    stats = functools.reduce(pooled, ring(stats, along_y))
    norm_s = stats[0] + jnp.log(stats[1])
    norm_t = stats[3] + jnp.log(stats[4])
    mean_gap = stats[2] / stats[1]
    kl_div = mean_gap - norm_s + norm_t
    rewards = norm_s - norm_t - stats[5]
    prob = jnp.exp(student - norm_s[:, None])
    grad = (prob * (gap - mean_gap[:, None])).astype(BF16)
    pieces = [grad[q, :, :quarter] for q in range(4)]
    return rewards, kl_div, jnp.concatenate(pieces, axis=1)


def solution(mesh):
    in_specs = (P("tv", "sv"), P("sv", "tv"), P("sv", "tv"), P("tv", "sv"), P("tv"))
    out_specs = (P("tv"), P("tv"), P("tv", "sv"))
    return jax.shard_map(shards, mesh=mesh, in_specs=in_specs, out_specs=out_specs, check_vma=False)
```

```python
import functools

import jax
import jax.numpy as jnp
from jax import lax
from jax.experimental import pallas as pl
from jax.experimental.pallas import tpu as pltpu
from jax.sharding import PartitionSpec as P

AXES = ("tv", "sv")
SHIFTS = (0, 1, 3, 2)
TILE = 256
F32 = jnp.float32
BF16 = jnp.bfloat16


def place(t, s):
    return t // 4, (t // 2) % 2, t % 2, s // 4, s % 4


def moved(x, step):
    pairs = []
    for source in range(128):
        z, xh, c, xl, y = step(*place(source // 8, source % 8))
        target = ((z % 4) * 4 + (xh % 2) * 2 + c % 2) * 8 + (xl % 2) * 4 + y % 4
        pairs.append((source, target))
    return lax.ppermute(x, AXES, pairs)


def along_z(d):
    return lambda z, xh, c, xl, y: (z + d, xh, c, xl, y)


def along_y(d):
    return lambda z, xh, c, xl, y: (z, xh, c, xl, y + d)


def other_core(z, xh, c, xl, y):
    return z, xh, c + 1, xl, y


def other_xh(z, xh, c, xl, y):
    return z, xh + 1, c, xl, y


def other_xl(z, xh, c, xl, y):
    return z, xh, c, xl + 1, y


def ring(x, along):
    return [x if d == 0 else moved(x, along(d)) for d in SHIFTS]


def ordered(parts, here):
    back = jnp.stack([parts[SHIFTS.index(d)] for d in (3, 2, 1, 0)] * 2)
    return lax.dynamic_slice_in_dim(back, 3 - here, 4, axis=0)


def paired(x, step, here, axis=0):
    other = moved(x, step)
    return jnp.where(
        here == 0, jnp.stack([x, other], axis=axis), jnp.stack([other, x], axis=axis)
    )


def coded(x):
    top = jnp.maximum(jnp.max(jnp.abs(x), axis=1, keepdims=True), 1e-30)
    power = jnp.ceil(jnp.log2(top) + 1e-4)
    code = jnp.clip(jnp.round(x * jnp.exp2(15.0 - power)), -32767.0, 32767.0)
    column = lax.broadcasted_iota(jnp.int32, x.shape, 1)
    return jnp.where(column == x.shape[1] - 1, power, code).astype(jnp.int16)


def decoded(code):
    power = code[:, -1:].astype(F32)
    return code.astype(F32) * jnp.exp2(power - 15.0)


def student_kernel(words, hidden, *refs):
    *weights, theirs, ours, joint = refs
    start = 0
    for w in weights:
        joint[start:start + w.shape[0], :] = w[...]
        start += w.shape[0]
    column = pl.program_id(0) * TILE + lax.broadcasted_iota(jnp.int32, ours.shape, 1)
    for part, out in ((1, theirs), (0, ours)):
        logits = jnp.dot(hidden[part], joint[...], preferred_element_type=F32)
        out[...] = jnp.where(column < words, logits, 0.0)


def student_partial(hidden, weights, first, words):
    _, rows, width = hidden.shape
    padded = (words // 128 + 1) * 128
    last = pl.cdiv(weights[0].shape[1], TILE) - 1
    block = pl.BlockSpec((rows, TILE), lambda j: (0, j))
    return pl.pallas_call(
        functools.partial(student_kernel, words),
        grid=(pl.cdiv(padded, TILE),),
        in_specs=[pl.BlockSpec((2, rows, width), lambda j: (0, 0, 0))]
        + [
            pl.BlockSpec((w.shape[0], TILE), lambda j: (0, jnp.minimum(j + first, last)))
            for w in weights
        ],
        out_specs=[block, block],
        out_shape=[jax.ShapeDtypeStruct((rows, padded), F32)] * 2,
        scratch_shapes=[pltpu.VMEM((width, TILE), BF16)],
        compiler_params=pltpu.CompilerParams(vmem_limit_bytes=40 << 20),
        cost_estimate=pl.CostEstimate(
            flops=4 * rows * width * words,
            bytes_accessed=2 * width * words + 8 * rows * words,
            transcendentals=0,
        ),
    )(hidden, *weights)


def teacher_kernel(hidden, weights, logits, total):
    k = pl.program_id(0)
    words = weights.shape[1]

    @pl.when(k == 0)
    def _():
        total[...] = jnp.zeros_like(total)

    total[:, :words] += lax.dot_general(
        hidden[0], weights[0], (((1,), (1,)), ((), ())), preferred_element_type=F32
    )

    @pl.when(k == pl.num_programs(0) - 1)
    def _():
        logits[...] = total[...]


def teacher_partial(hidden, weights, half, parts, padded):
    steps, rows, depth = hidden.shape
    words = weights.shape[1] // parts
    return pl.pallas_call(
        teacher_kernel,
        grid=(steps,),
        in_specs=[
            pl.BlockSpec((1, rows, depth), lambda k: (k, 0, 0)),
            pl.BlockSpec((1, words, depth), lambda k: (k, half, 0)),
        ],
        out_specs=pl.BlockSpec((rows, padded), lambda k: (0, 0)),
        out_shape=jax.ShapeDtypeStruct((rows, padded), F32),
        scratch_shapes=[pltpu.VMEM((rows, padded), F32)],
        compiler_params=pltpu.CompilerParams(vmem_limit_bytes=40 << 20),
        cost_estimate=pl.CostEstimate(
            flops=2 * steps * rows * depth * words,
            bytes_accessed=2 * steps * depth * (rows + words) + 4 * rows * padded,
            transcendentals=0,
        ),
    )(hidden, weights)


def student_rows(hidden, z, xh, c):
    rows = hidden.shape[2] // 2
    hidden = hidden.reshape(2, 2, 2, 2, rows, -1).transpose(3, 1, 2, 0, 4, 5)
    hidden = hidden.reshape(2, 2, 4, rows, -1)
    hidden = jnp.where(c == 0, hidden, hidden[::-1])
    hidden = jnp.where(xh == 0, hidden, hidden[:, ::-1])
    twice = jnp.concatenate([hidden, hidden], axis=2)
    hidden = lax.dynamic_slice_in_dim(twice, z, 4, axis=2)
    return hidden.reshape(2, 8 * rows, -1)


def student_piece(student_head, z, d, upper, lower):
    quarter = student_head.shape[1] // 4
    place = (upper, ((z + d) % 4) * quarter)
    return lax.dynamic_slice(student_head, place, (lower - upper, quarter))


def after(x, *others):
    return lax.optimization_barrier((x, others))[0]


def student_halves(ours, theirs):
    ours = ours + moved(theirs, other_core)
    half = ours.shape[0] // 2
    return ours[:half], coded(ours[half:])


def student_logits(ours, theirs):
    full = ours + decoded(theirs)
    rows = full.shape[0] // 4
    parts = [full[k * rows:(k + 1) * rows] for k in range(4)]
    return [parts[0]] + [moved(coded(parts[d]), along_z(d)) for d in SHIFTS[1:]]


def teacher_logits(ours, theirs):
    return (ours + decoded(theirs)).astype(BF16)


def over_tv(logits):
    rows = logits[0].shape[0] // 16
    logits = jnp.concatenate([part.reshape(16, rows, -1) for part in logits], axis=2)
    return lax.all_to_all(logits, "tv", 0, 0, tiled=True)


def over_sv(logits, chunk):
    _, rows, part = logits.shape
    logits = lax.all_to_all(logits.reshape(8, 2, rows, part), "sv", 0, 0, tiled=True)
    logits = logits.reshape(2, 4, 2, rows, 2, part // 2)[..., :chunk]
    return logits.transpose(2, 4, 3, 1, 0, 5).reshape(4, rows, 8 * chunk)


def halves(rows, chunk, xl):
    rows = rows.reshape(4, 2, chunk, -1)
    pair = [lax.dynamic_index_in_dim(rows, k, 1, keepdims=False) for k in (1 - xl, xl)]
    return [jnp.pad(half, ((0, 0), (0, -chunk % 16), (0, 0))) for half in pair]


def over_y(pieces):
    groups = [[0, 1, 2, 3], [4, 5, 6, 7]]
    return lax.all_to_all(pieces, "sv", 0, 0, axis_index_groups=groups, tiled=True)


def pooled(a, b):
    top_s = jnp.maximum(a[0], b[0])
    top_t = jnp.maximum(a[3], b[3])
    a_s, b_s = jnp.exp(a[0] - top_s), jnp.exp(b[0] - top_s)
    a_t, b_t = jnp.exp(a[3] - top_t), jnp.exp(b[3] - top_t)
    return jnp.stack([
        top_s,
        a[1] * a_s + b[1] * b_s,
        a[2] * a_s + b[2] * b_s,
        top_t,
        a[4] * a_t + b[4] * b_t,
        a[5] + b[5],
    ])


def shards(teacher_hidden, student_hidden, teacher_head, student_head, token_ids):
    t, s = lax.axis_index("tv"), lax.axis_index("sv")
    z, xh, c, xl, y = place(t, s)
    width = student_head.shape[1]
    quarter = width // 4
    chunk = -(-quarter // 64) * 8
    t_padded = (chunk // 128 + 1) * 128
    padded = -(-8 * chunk // 128) * 128
    split = -(-quarter // (2 * TILE))
    sizes = (split * TILE, quarter - split * TILE)
    rows, depth = teacher_hidden.shape
    pack = jnp.concatenate([teacher_hidden, student_hidden.reshape(-1, depth)])
    stage = ring(pack, along_z)
    t_first = jnp.concatenate(halves(teacher_head.T[:8 * chunk], chunk, xl), axis=1)
    height = student_head.shape[0]
    s_weights = [student_piece(student_head, z, d, 0, height) for d in SHIFTS[:3]]
    s_weights += [
        student_piece(student_head, z, SHIFTS[3], k * height // 2, (k + 1) * height // 2)
        for k in range(2)
    ]
    stage, t_first, s_weights = lax.optimization_barrier((stage, t_first, s_weights))

    t_first = over_y(t_first)
    s_weights[1] = moved(s_weights[1], along_z(SHIFTS[1]))
    s_weights[2] = moved(s_weights[2], along_z(SHIFTS[2]))
    s_hidden = [part[rows:].reshape(student_hidden.shape) for part in stage]
    s_hidden = paired(jnp.concatenate(s_hidden, axis=1), other_xl, xl)
    t_hidden = ordered([part[:rows] for part in stage], z)
    t_hidden = paired(t_hidden, other_xh, xh, axis=1)
    t_hidden = ordered(ring(t_hidden, along_y), y).reshape(32, rows, depth)
    t_hidden = paired(t_hidden, other_core, c, axis=1).reshape(4, 16 * rows, depth)
    t_hidden, s_hidden, teacher_head = lax.optimization_barrier((t_hidden, s_hidden, teacher_head))
    t_second = jnp.pad(teacher_head.T[quarter:], ((0, 8 * chunk - quarter), (0, 0)))
    t_second = halves(t_second, chunk, xl)

    s_hidden, s_weights[3] = after((s_hidden, s_weights[3]), t_first, s_weights[1], s_weights[2])
    s_hidden = over_y(jnp.broadcast_to(s_hidden[None], (4,) + s_hidden.shape))
    s_weights[3] = moved(s_weights[3], along_z(SHIFTS[3]))
    t_code = coded(teacher_partial(t_hidden, t_first, 0, 2, t_padded))
    t_ours = teacher_partial(t_hidden, t_first, 1, 2, t_padded)

    s_weights[4] = after(s_weights[4], s_hidden, s_weights[3], t_ours, t_code)
    t_theirs = over_y(after(t_second[0], s_hidden, s_weights[3], t_ours, t_code))
    t_second = over_y(after(t_second[1], t_theirs))
    s_weights[4] = moved(s_weights[4], along_z(SHIFTS[3]))
    t_first = teacher_logits(t_ours, moved(t_code, other_xl))
    s_hidden = student_rows(s_hidden, z, xh, c)

    s_hidden = after(s_hidden, t_theirs, t_first)
    s_theirs, s_ours = student_partial(s_hidden, s_weights, 0, sizes[0])
    s_first, first_code = student_halves(s_ours, s_theirs)
    t_code = coded(teacher_partial(t_hidden, t_theirs, 0, 1, t_padded))
    t_second = after(t_second, t_first, first_code, t_code)
    t_ours = teacher_partial(t_hidden, t_second, 0, 1, t_padded)
    t_second = teacher_logits(t_ours, moved(t_code, other_xl))
    s_weights = after(s_weights, t_second)
    teacher = over_tv([t_first, t_second])
    s_theirs, s_ours = student_partial(s_hidden, s_weights, split, sizes[1])
    s_second, second_code = student_halves(s_ours, s_theirs)
    first_code = moved(first_code, other_xh)
    teacher, first_code = after((teacher, first_code), teacher, second_code)
    teacher = over_sv(teacher, chunk)
    s_first = student_logits(s_first, first_code)
    s_second = student_logits(s_second, moved(second_code, other_xh))

    teacher = jnp.pad(teacher, ((0, 0), (0, 0), (0, padded - 8 * chunk))).astype(F32)
    student = jnp.zeros(teacher.shape, F32)
    for start, parts in ((0, s_first), (sizes[0], s_second)):
        for d, part in zip(SHIFTS, parts):
            part = part if d == 0 else decoded(part)
            part = part[:, :min(part.shape[1], sizes[0] if start == 0 else padded - start)]
            student = lax.dynamic_update_slice(student, part[None], ((z - d) % 4, 0, start))
    column = lax.broadcasted_iota(jnp.int32, student.shape, 2)
    index = lax.broadcasted_iota(jnp.int32, student.shape, 0) * quarter + column
    real = column < quarter
    student = jnp.where(real, student, -1e30)
    teacher = jnp.where(real, teacher, -1e30)
    gap = student - teacher
    chosen = real & (s * width + index == token_ids[:, None])
    picked = jnp.sum(jnp.where(chosen, gap, 0.0), axis=(0, 2))
    peak_s = jnp.max(student, axis=(0, 2))
    peak_t = jnp.max(teacher, axis=(0, 2))
    raw = jnp.exp(student - peak_s[:, None])
    mass_s = jnp.sum(raw, axis=(0, 2))
    mass_t = jnp.sum(jnp.exp(teacher - peak_t[:, None]), axis=(0, 2))
    cross = jnp.sum(raw * gap, axis=(0, 2))
    stats = jnp.stack([peak_s, mass_s, cross, peak_t, mass_t, picked])
    stats = pooled(stats, moved(stats, other_xl))
    stats = functools.reduce(pooled, ring(stats, along_y))
    norm_s = stats[0] + jnp.log(stats[1])
    norm_t = stats[3] + jnp.log(stats[4])
    mean_gap = stats[2] / stats[1]
    kl_div = mean_gap - norm_s + norm_t
    rewards = norm_s - norm_t - stats[5]
    prob = jnp.exp(student - norm_s[:, None])
    grad = (prob * (gap - mean_gap[:, None])).astype(BF16)
    pieces = [grad[q, :, :quarter] for q in range(4)]
    return rewards, kl_div, jnp.concatenate(pieces, axis=1)


def solution(mesh):
    in_specs = (P("tv", "sv"), P("sv", "tv"), P("sv", "tv"), P("tv", "sv"), P("tv"))
    out_specs = (P("tv"), P("tv"), P("tv", "sv"))
    return jax.shard_map(shards, mesh=mesh, in_specs=in_specs, out_specs=out_specs, check_vma=False)
```

```python
import functools

import jax
import jax.numpy as jnp
from jax import lax
from jax.experimental import pallas as pl
from jax.experimental.pallas import tpu as pltpu
from jax.sharding import PartitionSpec as P

AXES = ("tv", "sv")
SHIFTS = (0, 1, 3, 2)
TILE = 256
F32 = jnp.float32
BF16 = jnp.bfloat16


def place(t, s):
    return t // 4, (t // 2) % 2, t % 2, s // 4, s % 4


def moved(x, step):
    pairs = []
    for source in range(128):
        z, xh, c, xl, y = step(*place(source // 8, source % 8))
        target = ((z % 4) * 4 + (xh % 2) * 2 + c % 2) * 8 + (xl % 2) * 4 + y % 4
        pairs.append((source, target))
    return lax.ppermute(x, AXES, pairs)


def along_z(d):
    return lambda z, xh, c, xl, y: (z + d, xh, c, xl, y)


def along_y(d):
    return lambda z, xh, c, xl, y: (z, xh, c, xl, y + d)


def other_core(z, xh, c, xl, y):
    return z, xh, c + 1, xl, y


def other_xh(z, xh, c, xl, y):
    return z, xh + 1, c, xl, y


def other_xl(z, xh, c, xl, y):
    return z, xh, c, xl + 1, y


def ring(x, along):
    return [x if d == 0 else moved(x, along(d)) for d in SHIFTS]


def ordered(parts, here):
    back = jnp.stack([parts[SHIFTS.index(d)] for d in (3, 2, 1, 0)] * 2)
    return lax.dynamic_slice_in_dim(back, 3 - here, 4, axis=0)


def paired(x, step, here, axis=0):
    other = moved(x, step)
    return jnp.where(
        here == 0, jnp.stack([x, other], axis=axis), jnp.stack([other, x], axis=axis)
    )


def coded(x):
    top = jnp.maximum(jnp.max(jnp.abs(x), axis=1, keepdims=True), 1e-30)
    power = jnp.ceil(jnp.log2(top) + 1e-4)
    code = jnp.clip(jnp.round(x * jnp.exp2(15.0 - power)), -32767.0, 32767.0)
    column = lax.broadcasted_iota(jnp.int32, x.shape, 1)
    return jnp.where(column == x.shape[1] - 1, power, code).astype(jnp.int16)


def decoded(code):
    power = code[:, -1:].astype(F32)
    return code.astype(F32) * jnp.exp2(power - 15.0)


def student_kernel(words, hidden, *refs):
    *weights, theirs, ours, joint = refs
    start = 0
    for w in weights:
        joint[start:start + w.shape[0], :] = w[...]
        start += w.shape[0]
    column = pl.program_id(0) * TILE + lax.broadcasted_iota(jnp.int32, ours.shape, 1)
    for part, out in ((1, theirs), (0, ours)):
        logits = jnp.dot(hidden[part], joint[...], preferred_element_type=F32)
        out[...] = jnp.where(column < words, logits, 0.0)


def student_partial(hidden, weights):
    _, rows, width = hidden.shape
    words = weights[0].shape[1]
    padded = (words // 128 + 1) * 128
    last = pl.cdiv(words, TILE) - 1
    block = pl.BlockSpec((rows, TILE), lambda j: (0, j))
    return pl.pallas_call(
        functools.partial(student_kernel, words),
        grid=(pl.cdiv(padded, TILE),),
        in_specs=[pl.BlockSpec((2, rows, width), lambda j: (0, 0, 0))]
        + [
            pl.BlockSpec((w.shape[0], TILE), lambda j: (0, jnp.minimum(j, last)))
            for w in weights
        ],
        out_specs=[block, block],
        out_shape=[jax.ShapeDtypeStruct((rows, padded), F32)] * 2,
        scratch_shapes=[pltpu.VMEM((width, TILE), BF16)],
        compiler_params=pltpu.CompilerParams(vmem_limit_bytes=40 << 20),
        cost_estimate=pl.CostEstimate(
            flops=4 * rows * width * words,
            bytes_accessed=2 * width * words + 8 * rows * words,
            transcendentals=0,
        ),
    )(hidden, *weights)


def teacher_kernel(hidden, weights, logits, total):
    k = pl.program_id(0)
    words = weights.shape[1]

    @pl.when(k == 0)
    def _():
        total[...] = jnp.zeros_like(total)

    total[:, :words] += lax.dot_general(
        hidden[0], weights[0], (((1,), (1,)), ((), ())), preferred_element_type=F32
    )

    @pl.when(k == pl.num_programs(0) - 1)
    def _():
        logits[...] = total[...]


def teacher_partial(hidden, weights, half, parts, padded):
    steps, rows, depth = hidden.shape
    words = weights.shape[1] // parts
    return pl.pallas_call(
        teacher_kernel,
        grid=(steps,),
        in_specs=[
            pl.BlockSpec((1, rows, depth), lambda k: (k, 0, 0)),
            pl.BlockSpec((1, words, depth), lambda k: (k, half, 0)),
        ],
        out_specs=pl.BlockSpec((rows, padded), lambda k: (0, 0)),
        out_shape=jax.ShapeDtypeStruct((rows, padded), F32),
        scratch_shapes=[pltpu.VMEM((rows, padded), F32)],
        compiler_params=pltpu.CompilerParams(vmem_limit_bytes=40 << 20),
        cost_estimate=pl.CostEstimate(
            flops=2 * steps * rows * depth * words,
            bytes_accessed=2 * steps * depth * (rows + words) + 4 * rows * padded,
            transcendentals=0,
        ),
    )(hidden, weights)


def student_rows(hidden, z, xh, c):
    rows = hidden.shape[2] // 2
    hidden = hidden.reshape(2, 2, 2, 2, rows, -1).transpose(3, 1, 2, 0, 4, 5)
    hidden = hidden.reshape(2, 2, 4, rows, -1)
    hidden = jnp.where(c == 0, hidden, hidden[::-1])
    hidden = jnp.where(xh == 0, hidden, hidden[:, ::-1])
    twice = jnp.concatenate([hidden, hidden], axis=2)
    hidden = lax.dynamic_slice_in_dim(twice, z, 4, axis=2)
    return hidden.reshape(2, 8 * rows, -1)


def student_pieces(student_head, z, start, words):
    quarter = student_head.shape[1] // 4
    return [
        lax.dynamic_slice_in_dim(student_head, ((z + d) % 4) * quarter + start, words, axis=1)
        for d in SHIFTS
    ]


def after(x, *others):
    return lax.optimization_barrier((x, others))[0]


def student_halves(ours, theirs):
    ours = ours + moved(theirs, other_core)
    half = ours.shape[0] // 2
    return ours[:half], coded(ours[half:])


def student_logits(ours, theirs):
    full = ours + decoded(theirs)
    rows = full.shape[0] // 4
    parts = [full[k * rows:(k + 1) * rows] for k in range(4)]
    return [parts[0]] + [moved(coded(parts[d]), along_z(d)) for d in SHIFTS[1:]]


def teacher_logits(ours, theirs):
    return (ours + decoded(theirs)).astype(BF16)


def over_tv(logits):
    rows = logits[0].shape[0] // 16
    logits = jnp.concatenate([part.reshape(16, rows, -1) for part in logits], axis=2)
    return lax.all_to_all(logits, "tv", 0, 0, tiled=True)


def over_sv(logits, chunk):
    _, rows, part = logits.shape
    logits = lax.all_to_all(logits.reshape(8, 2, rows, part), "sv", 0, 0, tiled=True)
    pair = []
    for half in (logits[..., :part // 2], logits[..., part // 2:]):
        half = half.reshape(2, 4, 2, rows, part // 2)[..., :chunk].transpose(2, 3, 1, 0, 4)
        pair.append(half.reshape(2, rows, 8 * chunk))
    return jnp.stack(pair, axis=1).reshape(4, rows, 8 * chunk)


def halves(rows, chunk, xl):
    rows = rows.reshape(4, 2, chunk, -1)
    pair = [lax.dynamic_index_in_dim(rows, k, 1, keepdims=False) for k in (1 - xl, xl)]
    return [jnp.pad(half, ((0, 0), (0, -chunk % 16), (0, 0))) for half in pair]


def over_y(pieces):
    groups = [[0, 1, 2, 3], [4, 5, 6, 7]]
    return lax.all_to_all(pieces, "sv", 0, 0, axis_index_groups=groups, tiled=True)


def pooled(a, b):
    top_s = jnp.maximum(a[0], b[0])
    top_t = jnp.maximum(a[3], b[3])
    a_s, b_s = jnp.exp(a[0] - top_s), jnp.exp(b[0] - top_s)
    a_t, b_t = jnp.exp(a[3] - top_t), jnp.exp(b[3] - top_t)
    return jnp.stack([
        top_s,
        a[1] * a_s + b[1] * b_s,
        a[2] * a_s + b[2] * b_s,
        top_t,
        a[4] * a_t + b[4] * b_t,
        a[5] + b[5],
    ])


def shards(teacher_hidden, student_hidden, teacher_head, student_head, token_ids):
    t, s = lax.axis_index("tv"), lax.axis_index("sv")
    z, xh, c, xl, y = place(t, s)
    width = student_head.shape[1]
    quarter = width // 4
    chunk = -(-quarter // 64) * 8
    t_padded = (chunk // 128 + 1) * 128
    padded = -(-8 * chunk // 128) * 128
    split = -(-quarter // (2 * TILE))
    sizes = (split * TILE, quarter - split * TILE)
    rows, depth = teacher_hidden.shape
    pack = jnp.concatenate([teacher_hidden, student_hidden.reshape(-1, depth)])
    stage = ring(pack, along_z)
    t_first = jnp.concatenate(halves(teacher_head.T[:8 * chunk], chunk, xl), axis=1)
    s_first = student_pieces(student_head, z, 0, sizes[0])
    stage, t_first, s_first = lax.optimization_barrier((stage, t_first, s_first))

    t_first = over_y(t_first)
    s_first[1] = moved(s_first[1], along_z(SHIFTS[1]))
    s_first[2] = moved(s_first[2], along_z(SHIFTS[2]))
    s_first[3] = moved(after(s_first[3], s_first[1], s_first[2]), along_z(SHIFTS[3]))
    s_hidden = [part[rows:].reshape(student_hidden.shape) for part in stage]
    s_hidden = paired(jnp.concatenate(s_hidden, axis=1), other_xl, xl)
    t_hidden = ordered([part[:rows] for part in stage], z)
    t_hidden = paired(t_hidden, other_xh, xh, axis=1)
    t_hidden, student_head = after(
        (ring(t_hidden, along_y), student_head), s_first[1], s_first[2]
    )
    s_second = student_pieces(student_head, z, sizes[0], sizes[1])
    t_hidden = ordered(t_hidden, y).reshape(32, rows, depth)
    t_hidden = paired(after(t_hidden, s_second), other_core, c, axis=1).reshape(4, 16 * rows, depth)
    t_hidden, s_hidden, teacher_head = lax.optimization_barrier((t_hidden, s_hidden, teacher_head))
    t_second = jnp.pad(teacher_head.T[quarter:], ((0, 8 * chunk - quarter), (0, 0)))
    t_second = halves(t_second, chunk, xl)

    s_hidden, s_second = after((s_hidden, s_second), t_first, s_first)
    s_hidden = over_y(jnp.broadcast_to(s_hidden[None], (4,) + s_hidden.shape))
    s_second[1] = moved(s_second[1], along_z(SHIFTS[1]))
    s_second[2] = moved(s_second[2], along_z(SHIFTS[2]))
    t_code = coded(teacher_partial(t_hidden, t_first, 0, 2, t_padded))
    t_ours = teacher_partial(t_hidden, t_first, 1, 2, t_padded)

    s_second[3], t_theirs = after(
        (s_second[3], t_second[0]), s_hidden, s_second[1], s_second[2], t_ours, t_code
    )
    t_theirs = over_y(t_theirs)
    s_second[3] = moved(s_second[3], along_z(SHIFTS[3]))
    t_first = teacher_logits(t_ours, moved(t_code, other_xl))
    s_hidden = after(s_hidden, s_second[1], s_second[2], t_ours, t_first, t_second)
    s_hidden = student_rows(s_hidden, z, xh, c)
    theirs, ours = student_partial(s_hidden, s_first)
    t_second = over_y(after(t_second[1], t_theirs, theirs, t_first))
    s_first, first_code = student_halves(ours, theirs)

    t_code = coded(teacher_partial(t_hidden, t_theirs, 0, 1, t_padded))
    first_code = moved(first_code, other_xh)
    t_code = moved(after(t_code, first_code), other_xl)
    t_ours = teacher_partial(t_hidden, after(t_second, t_code), 0, 1, t_padded)
    t_second = teacher_logits(t_ours, t_code)
    teacher = over_tv([t_first, t_second])
    theirs, ours = student_partial(s_hidden, after(s_second, t_ours))
    s_second, code = student_halves(ours, theirs)
    s_first = student_logits(after(s_first, code), first_code)
    teacher = over_sv(after(teacher, code), chunk)
    s_second = student_logits(s_second, moved(code, other_xh))

    teacher = jnp.pad(teacher, ((0, 0), (0, 0), (0, padded - 8 * chunk))).astype(F32)
    student = jnp.zeros(teacher.shape, F32)
    for start, parts in ((0, s_first), (sizes[0], s_second)):
        for d, part in zip(SHIFTS, parts):
            part = part if d == 0 else decoded(part)
            part = part[:, :min(part.shape[1], sizes[0] if start == 0 else padded - start)]
            student = lax.dynamic_update_slice(student, part[None], ((z - d) % 4, 0, start))
    column = lax.broadcasted_iota(jnp.int32, student.shape, 2)
    index = lax.broadcasted_iota(jnp.int32, student.shape, 0) * quarter + column
    real = column < quarter
    student = jnp.where(real, student, -1e30)
    teacher = jnp.where(real, teacher, -1e30)
    gap = student - teacher
    chosen = real & (s * width + index == token_ids[:, None])
    picked = jnp.sum(jnp.where(chosen, gap, 0.0), axis=(0, 2))
    peak_s = jnp.max(student, axis=(0, 2))
    peak_t = jnp.max(teacher, axis=(0, 2))
    raw = jnp.exp(student - peak_s[:, None])
    mass_s = jnp.sum(raw, axis=(0, 2))
    mass_t = jnp.sum(jnp.exp(teacher - peak_t[:, None]), axis=(0, 2))
    cross = jnp.sum(raw * gap, axis=(0, 2))
    stats = jnp.stack([peak_s, mass_s, cross, peak_t, mass_t, picked])
    stats = pooled(stats, moved(stats, other_xl))
    stats = functools.reduce(pooled, ring(stats, along_y))
    norm_s = stats[0] + jnp.log(stats[1])
    norm_t = stats[3] + jnp.log(stats[4])
    mean_gap = stats[2] / stats[1]
    kl_div = mean_gap - norm_s + norm_t
    rewards = norm_s - norm_t - stats[5]
    prob = jnp.exp(student - norm_s[:, None])
    grad = (prob * (gap - mean_gap[:, None])).astype(BF16)
    pieces = [grad[q, :, :quarter] for q in range(4)]
    return rewards, kl_div, jnp.concatenate(pieces, axis=1)


def solution(mesh):
    in_specs = (P("tv", "sv"), P("sv", "tv"), P("sv", "tv"), P("tv", "sv"), P("tv"))
    out_specs = (P("tv"), P("tv"), P("tv", "sv"))
    return jax.shard_map(shards, mesh=mesh, in_specs=in_specs, out_specs=out_specs, check_vma=False)
```
